512 devices in a mesh: dp: 32 (over z, x), fsdp: 16 (over y, core).
Axes of the slice: x: 4, y: 8, z: 8, core: 2. Of those that a mesh axis runs over, the one named last changes fastest.
Arguments:
- momentum: float32 [32, 2, 1048576], P('dp', None, 'fsdp'), may hold values from -6 to 6
- gradients: bfloat16 [32, 2, 1048576], P('dp', None, 'fsdp'), may hold values from -6 to 6
- weight: bfloat16 [2, 1048576], P(None, 'fsdp'), may hold values from -2 to 2
- indices: int32 [32, 2, 4, 16384], P('dp', None, None, 'fsdp'), may hold values from 0 to 63, as said below
Outputs:
- moment_out: float32 [32, 2, 1048576], P('dp', None, 'fsdp')
- weight_out: bfloat16 [2, 1048576], replicated
The draws below stay inside these ranges and needn't reach their ends.
Inputs may be any that keep to these rules, and one draw needn't show every extreme that they name: `indices`: for every replica, tensor and block the 4 components differ.
All inputs are finite; a program needn't handle non-finite values.
Results may differ from the reference program's by a relative error of at most 0.001.
Values may be sent and summed in bfloat16 or wider, within the bound.
A program may use at most 64 MiB of HBM per device.

```python
import math
import jax
import jax.numpy as jnp
from jax import lax

STRETCH = 64
TOPK = 4
LAYERS = 2
SPAN = 1048576
REPLICAS = 32


def draw_indices(key, part):
    key = jax.random.fold_in(key, 7)
    scores = jax.random.randint(key, (REPLICAS, LAYERS, SPAN // STRETCH, STRETCH), 0, 2 ** 20, dtype=jnp.int32)
    scores = scores * STRETCH + jnp.arange(STRETCH, dtype=jnp.int32)
    chosen = lax.top_k(scores, TOPK)[1]
    return jnp.swapaxes(chosen, 2, 3).astype(jnp.int32)


def steps_of(rng, dims, shards, smallest, largest):
    factor_of = 1.0
    for position, blocks in shards:
        heights = jax.random.uniform(jax.random.fold_in(jax.random.fold_in(rng, 6), position), (blocks,), jnp.float32, smallest / len(shards), largest / len(shards))
        factor_of = factor_of * jnp.repeat(jnp.exp(heights), dims[position] // blocks).reshape((-1,) + (1,) * (len(dims) - 1 - position))
    return factor_of


def bell_draw(rng, shape, deviation, limit, shards=(), kind=jnp.bfloat16):
    gain = steps_of(rng, shape, shards, -0.22, 0.18) if shards else 1.0
    result = jax.random.normal(rng, shape, jnp.float32) * deviation * gain
    return jnp.minimum(jnp.maximum(result, -limit), limit).astype(kind)


def setup_inputs(seed: int = 0) -> dict:
    keys = jax.random.split(jax.random.key(seed), 5)
    return {
        "momentum": bell_draw(keys[0], (REPLICAS, LAYERS, SPAN), 1.0, 6.0, ((0, 32), (2, 16)), jnp.float32),
        "gradients": bell_draw(keys[1], (REPLICAS, LAYERS, SPAN), 1.0, 6.0, ((0, 32), (2, 16))),
        "weight": bell_draw(keys[2], (LAYERS, SPAN), 0.25, 2.0, ((1, 16),)),
        "indices": draw_indices(jax.random.fold_in(keys[4], 71), 0),
    }


decay_rate = 0.999
rate_step = 0.125

def cosine_table():
    rows_k = jnp.arange(STRETCH, dtype=jnp.float32)[:, None]
    cols_n = jnp.arange(STRETCH, dtype=jnp.float32)[None, :]
    weights_k = jnp.where(rows_k == 0, math.sqrt(1.0 / STRETCH), math.sqrt(2.0 / STRETCH))
    return weights_k * jnp.cos(math.pi * (2.0 * cols_n + 1.0) * rows_k / (2.0 * STRETCH))

def reference(momentum, gradients, weight, indices):
    cosine = cosine_table()
    driven = decay_rate * momentum + gradients.astype(jnp.float32)
    blocks = driven.reshape(REPLICAS, LAYERS, SPAN // STRETCH, STRETCH)
    spectrum = jnp.einsum('rlcn,kn->rlck', blocks, cosine, precision=lax.Precision.HIGHEST)
    components = jnp.arange(STRETCH, dtype=jnp.int32)
    dense = jnp.zeros_like(spectrum)
    for slot_index in range(TOPK):
        target = indices[:, :, slot_index, :][..., None]
        matches = components == target
        picked = lax.optimization_barrier(jnp.sum(jnp.where(matches, spectrum, jnp.zeros_like(spectrum)), axis=-1, keepdims=True))
        dense = dense + jnp.where(matches, picked, jnp.zeros_like(spectrum))
    own_back = jnp.einsum('rlck,kn->rlcn', dense, cosine, precision=lax.Precision.HIGHEST)
    moment_out = driven - own_back.reshape(REPLICAS, LAYERS, SPAN)
    summed = lax.optimization_barrier(jnp.sum(dense, axis=0))
    restored = jnp.einsum('lck,kn->lcn', summed, cosine, precision=lax.Precision.HIGHEST).reshape(LAYERS, SPAN)
    weight_out = (weight.astype(jnp.float32) - rate_step * restored).astype(jnp.bfloat16)
    return (moment_out, weight_out)
```

```python
import math

import jax
import jax.numpy as jnp
import numpy as np
from jax import lax
from jax.experimental import pallas as pl
from jax.experimental.pallas import tpu as pltpu
from jax.sharding import PartitionSpec as P

STRETCH = 64
TOPK = 4
NX, NY, NZ = 4, 8, 8
COLOURS = 8
ROWS = 128

decay_rate = 0.999
rate_step = 0.125

ALIKE = ((1, 1, -1), (-1, -1, 1), (-1, 2, 0), (1, -2, 0), (0, 3, -1), (0, -3, 1), (2, 4, 0))
AROUND = ((1, 0, 0), (-1, 0, 0), (0, 1, 0), (0, -1, 0), (0, 0, 1), (0, 0, -1))
ACROSS = ((0, 1, 1), (0, -1, -1)) + 6 * ((2, 0, 0),)


def pair_table():
    k = np.arange(STRETCH, dtype=np.float64)[:, None]
    n = np.arange(STRETCH, dtype=np.float64)[None, :]
    scale = np.where(k == 0, math.sqrt(1.0 / STRETCH), math.sqrt(2.0 / STRETCH))
    cosine = scale * np.cos(math.pi * (2.0 * n + 1.0) * k / (2.0 * STRETCH))
    return np.kron(np.eye(2), cosine).astype(np.float32)


def iota(shape, dim):
    return lax.broadcasted_iota(jnp.int32, shape, dim)


def exact_dot(a, b):
    return jnp.dot(a, b, precision=lax.Precision.HIGHEST, preferred_element_type=jnp.float32)


def lane_gather(values, lanes):
    return jnp.take_along_axis(values, lanes, axis=1, mode="promise_in_bounds")


def spread(packed, piece, slot):
    return lane_gather(packed, 8 * piece + 2 * slot + iota((8, 128), 1) // STRETCH)


def transform_kernel(momentum, gradients, indices, forward, backward, moment_out, message):
    lane = iota((8, 128), 1)
    row = iota((8, 128), 0)
    deep_row = iota((128, 128), 0)
    deep_lane = iota((128, 128), 1)

    packed = jnp.zeros((8 * COLOURS, 128), jnp.float32)
    mine = (lane // 2) % 4 == row // 2
    for slot in range(TOPK):
        tiles = []
        for share in range(COLOURS):
            columns = pl.ds(128 * share, 128)
            first = indices[pl.ds(slot, 1), columns]
            second = indices[pl.ds(TOPK + slot, 1), columns]
            both = jnp.where(row % 2 == 0, first, second)
            tiles.append(jnp.where(mine, both, 0).astype(jnp.float32))
        place = (deep_row // 8 == deep_lane // 8) & (deep_row % 2 == deep_lane % 2) & ((deep_lane // 2) % 4 == slot)
        packed = packed + jnp.dot(
            jnp.concatenate(tiles, axis=0).astype(jnp.bfloat16),
            jnp.where(place, 1.0, 0.0).astype(jnp.bfloat16),
            preferred_element_type=jnp.float32,
        )

    component = (lane % STRETCH).astype(jnp.float32)
    for share in range(COLOURS):
        rows = pl.ds(ROWS * share, ROWS)
        driven = decay_rate * momentum[rows, :] + gradients[rows, :].astype(jnp.float32)
        spectrum = exact_dot(driven, forward[...])
        places = packed[8 * share : 8 * share + 8]
        lanes = places.astype(jnp.int32) + STRETCH * (lane % 2)
        values = jnp.zeros((8, 128), jnp.float32)
        dense = []
        for piece in range(16):
            part = spectrum[8 * piece : 8 * piece + 8]
            values = jnp.where(lane // 8 == piece, lane_gather(part, lanes), values)
            kept = spread(places, piece, 0) == component
            for slot in range(1, TOPK):
                kept = kept | (spread(places, piece, slot) == component)
            dense.append(jnp.where(kept, part, 0.0))
        message[share, pl.ds(0, 8), :] = values
        message[share, pl.ds(8, 8), :] = places
        moment_out[rows, :] = driven - exact_dot(jnp.concatenate(dense, axis=0), backward[...])


def share_kernel(message, weight, backward, whole, inbox, total, list_sent, list_here, alike_sent, alike_here,
                 around_sent, around_here, twin_sent, twin_here):
    dp = lax.axis_index("dp")
    fsdp = lax.axis_index("fsdp")
    z, x = dp // NX, dp % NX
    y, core = fsdp // 2, fsdp % 2
    colour = (2 * x + y + 3 * z) % COLOURS

    def chip(dx, dy, dz):
        return (((z + dz + NZ) % NZ) * NX + (x + dx + NX) % NX, ((y + dy + NY) % NY) * 2 + core)

    twin = (dp, y * 2 + 1 - core)

    def plane_step(which):
        turn = which // NX
        dz = jnp.where(turn % 2 == 1, (turn + 1) // 2, (NZ - turn // 2) % NZ)
        return which % NX, dz

    barrier = pltpu.get_barrier_semaphore()

    def greet(which, carry):
        dx, dz = plane_step(which)
        pl.semaphore_signal(barrier, 1, device_id=chip(-dx, 0, -dz))
        return carry

    lax.fori_loop(1, NX * NZ, greet, 0)
    others = sorted(set(ALIKE + AROUND + ACROSS))
    for dx, dy, dz in others:
        pl.semaphore_signal(barrier, 1, device_id=chip(-dx, -dy, -dz))
    pl.semaphore_signal(barrier, 1, device_id=twin)
    pl.semaphore_wait(barrier, NX * NZ - 1 + len(others) + 1)

    def send_list(step, carry):
        which = NX * NZ - 1 - step
        dx, dz = plane_step(which)
        theirs = (colour + 2 * dx + 3 * dz) % COLOURS
        pltpu.make_async_remote_copy(
            src_ref=message.at[theirs], dst_ref=inbox.at[which], send_sem=list_sent,
            recv_sem=list_here.at[which], device_id=chip(dx, 0, dz),
        ).start()
        return carry

    lax.fori_loop(0, NX * NZ - 1, send_list, 0)

    lane = iota((8, 128), 1)
    component = (lane % STRETCH).astype(jnp.float32)

    def add_list(values, places, first):
        for piece in range(16):
            rows = pl.ds(8 * piece, 8)
            summed = jnp.zeros((8, 128), jnp.float32) if first else total[rows, :]
            for slot in range(TOPK):
                kept = spread(places, piece, slot) == component
                summed = summed + jnp.where(kept, spread(values, piece, slot), 0.0)
            total[rows, :] = summed

    add_list(message[colour, pl.ds(0, 8), :], message[colour, pl.ds(8, 8), :], True)

    def take_list(which, carry):
        pltpu.make_async_copy(inbox.at[which], inbox.at[which], list_here.at[which]).wait()
        add_list(inbox[which, pl.ds(0, 8), :], inbox[which, pl.ds(8, 8), :], False)
        return carry

    lax.fori_loop(1, NX * NZ, take_list, 0)

    restored = exact_dot(total[...], backward[...])
    own = weight[pl.ds(pl.multiple_of(colour * ROWS, ROWS), ROWS), :].astype(jnp.float32)
    whole[y, core, colour] = (own - rate_step * restored).astype(jnp.bfloat16)

    def block(plane, parity, tint):
        return whole.at[plane, parity, tint]

    def to_twin(plane, tint):
        pltpu.make_async_remote_copy(
            src_ref=block(plane, core, tint), dst_ref=block(plane, core, tint), send_sem=twin_sent,
            recv_sem=twin_here, device_id=twin,
        ).start()

    def pass_on(plane, number):
        for way, step in enumerate(AROUND + (ACROSS[number],)):
            pltpu.make_async_remote_copy(
                src_ref=block(plane, core, colour), dst_ref=block(plane, core, colour),
                send_sem=around_sent, recv_sem=around_here.at[way, number], device_id=chip(*step),
            ).start()
        to_twin(plane, colour)

    def await_block(plane, tint, semaphore):
        pltpu.make_async_copy(block(plane, core, tint), block(plane, core, tint), semaphore).wait()

    for number in reversed(range(len(ALIKE))):
        pltpu.make_async_remote_copy(
            src_ref=block(y, core, colour), dst_ref=block(y, core, colour), send_sem=alike_sent,
            recv_sem=alike_here.at[number], device_id=chip(*ALIKE[number]),
        ).start()
    pass_on(y, 0)
    for number, step in enumerate(ALIKE):
        plane = (y - step[1] + NY) % NY
        await_block(plane, colour, alike_here.at[number])
        pass_on(plane, number + 1)

    for number in range(NY):
        back = 0 if number == 0 else ALIKE[number - 1][1]
        for way, step in enumerate(AROUND + (ACROSS[number],)):
            plane = (y - step[1] - back + 2 * NY) % NY
            tint = (colour - 2 * step[0] - step[1] - 3 * step[2] + 2 * COLOURS) % COLOURS
            await_block(plane, tint, around_here.at[way, number])
            to_twin(plane, tint)

    def await_bytes(ref, semaphore):
        pltpu.make_async_copy(ref, ref, semaphore).wait()

    await_bytes(inbox.at[pl.ds(1, NX * NZ - 1)], list_sent)
    await_bytes(whole.at[pl.ds(0, 7), core, 0], alike_sent)
    await_bytes(whole.at[pl.ds(0, 7), core], around_sent)
    await_bytes(whole.at[:, core], twin_sent)
    await_bytes(whole.at[:, 1 - core], twin_here)


def as_rows(array):
    layers, entries = array.shape
    return array.reshape(layers, entries // 128, 128).transpose(1, 0, 2).reshape(layers * entries // 128, 128)


def from_rows(array, layers):
    pieces = array.shape[0] // layers
    return array.reshape(pieces, layers, 128).transpose(1, 0, 2).reshape(layers, pieces * 128)


def shards(momentum, gradients, weight, indices):
    layers, entries = weight.shape
    table = pair_table()
    forward, backward = jnp.asarray(table.T), jnp.asarray(table)
    in_vmem = pl.BlockSpec(memory_space=pltpu.VMEM)
    moment_rows, message = pl.pallas_call(
        transform_kernel,
        out_shape=(
            jax.ShapeDtypeStruct((layers * entries // 128, 128), jnp.float32),
            jax.ShapeDtypeStruct((COLOURS, 16, 128), jnp.float32),
        ),
        in_specs=[in_vmem] * 5,
        out_specs=(in_vmem, in_vmem),
        compiler_params=pltpu.CompilerParams(vmem_limit_bytes=24 * 2**20),
    )(as_rows(momentum[0]), as_rows(gradients[0]), indices.reshape(layers * TOPK, -1), forward, backward)
    dma = pltpu.SemaphoreType.DMA
    whole = pl.pallas_call(
        share_kernel,
        out_shape=jax.ShapeDtypeStruct((NY, 2, COLOURS, ROWS, 128), jnp.bfloat16),
        in_specs=[in_vmem] * 3,
        out_specs=in_vmem,
        scratch_shapes=[
            pltpu.VMEM((NX * NZ, 16, 128), jnp.float32),
            pltpu.VMEM((ROWS, 128), jnp.float32),
            dma, dma((NX * NZ,)), dma, dma((len(ALIKE),)), dma, dma((7, NY)), dma, dma,
        ],
        compiler_params=pltpu.CompilerParams(
            collective_id=0, has_side_effects=True, vmem_limit_bytes=24 * 2**20
        ),
    )(message, as_rows(weight), backward)
    weight_out = from_rows(whole.reshape(-1, 128), layers)
    return (from_rows(moment_rows, layers)[None], weight_out)


def solution(mesh):
    return jax.shard_map(
        shards,
        mesh=mesh,
        in_specs=(
            P("dp", None, "fsdp"),
            P("dp", None, "fsdp"),
            P(None, "fsdp"),
            P("dp", None, None, "fsdp"),
        ),
        out_specs=(P("dp", None, "fsdp"), P()),
        check_vma=False,
    )
```

```python
import math

import jax
import jax.numpy as jnp
import numpy as np
from jax import lax
from jax.experimental import pallas as pl
from jax.experimental.pallas import tpu as pltpu
from jax.sharding import PartitionSpec as P

STRETCH = 64
TOPK = 4
NX, NY, NZ = 4, 8, 8
COLOURS = 8
ROWS = 128

decay_rate = 0.999
rate_step = 0.125

ALIKE = ((1, 1, -1), (-1, -1, 1), (-1, 2, 0), (1, -2, 0), (0, 3, -1), (0, -3, 1), (2, 4, 0))
AROUND = ((1, 0, 0), (-1, 0, 0), (0, 1, 0), (0, -1, 0), (0, 0, 1), (0, 0, -1))
ACROSS = ((0, 1, 1), (0, -1, -1)) + 6 * ((2, 0, 0),)


def pair_tables():
    k = np.arange(STRETCH, dtype=np.float64)[:, None]
    n = np.arange(STRETCH, dtype=np.float64)[None, :]
    scale = np.where(k == 0, math.sqrt(1.0 / STRETCH), math.sqrt(2.0 / STRETCH))
    cosine = np.kron(np.eye(2), scale * np.cos(math.pi * (2.0 * n + 1.0) * k / (2.0 * STRETCH)))

    return np.stack([cosine.T, cosine]).astype(np.float32)


def iota(shape, dim):
    return lax.broadcasted_iota(jnp.int32, shape, dim)


def lane_gather(values, lanes):
    return jnp.take_along_axis(values, lanes, axis=1, mode="promise_in_bounds")


def split(values):
    high = values.astype(jnp.bfloat16)
    low = (values - high.astype(jnp.float32)).astype(jnp.bfloat16)
    return jnp.concatenate([high, low], axis=1)


def table_dot(rows, table):
    both = jnp.dot(
        split(rows),
        jnp.concatenate([table, table], axis=0),
        preferred_element_type=jnp.float32,
    )
    return both[:, :128] + both[:, 128:]


def sync_kernel(momentum_in, gradients_in, weight_in, indices_in, tables_in, moment_out, whole,
                momentum, gradients, weight, indices, tables, kept_columns, message, inbox, loaded,
                list_sent, list_here, alike_sent, alike_here, around_sent, around_here, twin_sent, twin_here):
    dp = lax.axis_index("dp")
    fsdp = lax.axis_index("fsdp")
    z, x = lax.div(dp, NX), lax.rem(dp, NX)
    y, core = lax.div(fsdp, 2), lax.rem(fsdp, 2)
    colour = lax.rem(2 * x + y + 3 * z, COLOURS)
    xs = [lax.rem(x + d, NX) for d in range(NX)]
    ys = [lax.rem(y + d, NY) for d in range(NY)]
    zs = [lax.rem(z + d, NZ) for d in range(NZ)]
    tints = [lax.rem(colour + d, COLOURS) for d in range(COLOURS)]

    def chip(dx, dy, dz):
        return (zs[dz % NZ] * NX + xs[dx % NX], ys[dy % NY] * 2 + core)

    twin = (dp, y * 2 + 1 - core)

    own_rows = pl.ds(pl.multiple_of(colour * ROWS, ROWS), ROWS)
    loads = [
        pltpu.make_async_copy(source, target, loaded.at[number])
        for number, (source, target) in enumerate((
            (indices_in, indices), (tables_in, tables), (momentum_in, momentum),
            (gradients_in, gradients), (weight_in.at[own_rows], weight),
        ))
    ]
    for load in loads:
        load.start()

    plane = [(dx, dz) for dz in (4, 3, 5, 2, 6, 1, 7, 0) for dx in (2, 1, 3, 0) if (dx, dz) != (0, 0)]
    barrier = pltpu.get_barrier_semaphore()
    for dx, dz in plane:
        pl.semaphore_signal(barrier, 1, device_id=chip(dx, 0, dz))
    others = sorted(set(ALIKE + AROUND + ACROSS) - {(dx, 0, dz) for dx, dy, dz in AROUND if dy == 0} - {(2, 0, 0)})
    for dx, dy, dz in others:
        pl.semaphore_signal(barrier, 1, device_id=chip(-dx, -dy, -dz))
    pl.semaphore_signal(barrier, 1, device_id=twin)

    lane = iota((8, 128), 1)
    even = iota((TOPK, 128), 1) % 2 == 0
    component = iota((STRETCH, 128), 0)

    for load in loads[:4]:
        load.wait()

    forward, backward = split(tables[0]), split(tables[1])

    def driven_rows(rows):
        return decay_rate * momentum[rows, :] + gradients[rows, :].astype(jnp.float32)

    def transform(share, carry):
        rows = pl.ds(pl.multiple_of(share * ROWS, ROWS), ROWS)
        columns = table_dot(driven_rows(rows), forward).T
        listed = jnp.concatenate([indices[0, :, rows], indices[1, :, rows]], axis=0)
        below = lane_gather(listed, (lane + 127) % 128)
        above = lane_gather(listed, (lane + 1) % 128)
        places = (
            jnp.where(even, listed[:TOPK], below[TOPK:]),
            jnp.where(even, above[:TOPK], listed[TOPK:]),
        )
        for half in range(2):
            part = columns[STRETCH * half : STRETCH * (half + 1)]
            kept = jnp.zeros((STRETCH, 128), jnp.float32)
            for slot in range(TOPK):
                match = component == places[half][slot : slot + 1]
                picked = jnp.where(match, part, 0.0)
                message[share, half, pl.ds(slot, 1), :] = jnp.sum(picked, axis=0, keepdims=True)
                kept = jnp.where(match, part, kept)
            kept_columns[share, pl.ds(STRETCH * half, STRETCH), :] = kept
        message[share, 2] = (places[0] + 65536 * places[1]).astype(jnp.float32)
        return carry

    lax.fori_loop(0, COLOURS, transform, 0)

    pl.semaphore_wait(barrier, len(plane) + len(others) + 1)

    for number, (dx, dz) in enumerate(plane):
        pltpu.make_async_remote_copy(
            src_ref=message.at[tints[(2 * dx + 3 * dz) % COLOURS]], dst_ref=inbox.at[number], send_sem=list_sent,
            recv_sem=list_here.at[number], device_id=chip(dx, 0, dz),
        ).start()

    def keep_rest(share, carry):
        rows = pl.ds(pl.multiple_of(share * ROWS, ROWS), ROWS)
        moment_out[rows, :] = driven_rows(rows) - table_dot(kept_columns[share].T, backward)
        return carry

    lax.fori_loop(0, COLOURS, keep_rest, 0)

    def add_list(number, summed):
        pltpu.make_async_copy(inbox.at[number], inbox.at[number], list_here.at[number]).wait()
        coded = inbox[number, 2].astype(jnp.int32)
        places = (coded % 65536, coded // 65536)
        halves = []
        for half in range(2):
            term = jnp.zeros((STRETCH, 128), jnp.float32)
            for slot in range(TOPK):
                match = component == places[half][slot : slot + 1]
                term = jnp.where(match, inbox[number, half, pl.ds(slot, 1), :], term)
            halves.append(summed[STRETCH * half : STRETCH * (half + 1)] + term)
        return jnp.concatenate(halves, axis=0)

    summed = lax.fori_loop(0, len(plane), add_list, kept_columns[colour])
    restored = table_dot(summed.T, backward)
    loads[4].wait()
    whole[y, core, colour] = (weight[...].astype(jnp.float32) - rate_step * restored).astype(jnp.bfloat16)

    def block(plane, tint):
        return whole.at[plane, core, tint]

    def to_twin(plane, tint):
        pltpu.make_async_remote_copy(
            src_ref=block(plane, tint), dst_ref=block(plane, tint), send_sem=twin_sent,
            recv_sem=twin_here, device_id=twin,
        ).start()

    def pass_on(plane, number):
        for way, step in enumerate(AROUND + (ACROSS[number],)):
            pltpu.make_async_remote_copy(
                src_ref=block(plane, colour), dst_ref=block(plane, colour),
                send_sem=around_sent, recv_sem=around_here.at[way, number], device_id=chip(*step),
            ).start()
        to_twin(plane, colour)

    def await_block(plane, tint, semaphore):
        pltpu.make_async_copy(block(plane, tint), block(plane, tint), semaphore).wait()

    for number in reversed(range(len(ALIKE))):
        pltpu.make_async_remote_copy(
            src_ref=block(y, colour), dst_ref=block(y, colour), send_sem=alike_sent,
            recv_sem=alike_here.at[number], device_id=chip(*ALIKE[number]),
        ).start()
    pass_on(y, 0)
    for number, step in enumerate(ALIKE):
        there = ys[-step[1] % NY]
        await_block(there, colour, alike_here.at[number])
        pass_on(there, number + 1)

    for number in range(NY):
        back = 0 if number == 0 else ALIKE[number - 1][1]
        for way, step in enumerate(AROUND + (ACROSS[number],)):
            there = ys[(-step[1] - back) % NY]
            tint = tints[-(2 * step[0] + step[1] + 3 * step[2]) % COLOURS]
            await_block(there, tint, around_here.at[way, number])
            to_twin(there, tint)

    def await_bytes(ref, semaphore):
        pltpu.make_async_copy(ref, ref, semaphore).wait()

    await_bytes(inbox, list_sent)
    await_bytes(whole.at[pl.ds(0, 7), core, 0], alike_sent)
    await_bytes(whole.at[pl.ds(0, 7), core], around_sent)
    await_bytes(whole.at[:, core], twin_sent)
    await_bytes(whole.at[:, 1 - core], twin_here)


def as_rows(array):
    layers, entries = array.shape
    return array.reshape(layers, entries // 128, 128).transpose(1, 0, 2).reshape(layers * entries // 128, 128)


def from_rows(array, layers):
    pieces = array.shape[0] // layers
    return array.reshape(pieces, layers, 128).transpose(1, 0, 2).reshape(layers, pieces * 128)


def shards(momentum, gradients, weight, indices):
    layers, entries = weight.shape
    rows = layers * entries // 128
    in_hbm = pl.BlockSpec(memory_space=pltpu.HBM)
    in_vmem = pl.BlockSpec(memory_space=pltpu.VMEM)
    dma = pltpu.SemaphoreType.DMA
    peers = NX * NZ - 1
    operands = (
        as_rows(momentum[0]), as_rows(gradients[0]), as_rows(weight), indices[0], jnp.asarray(pair_tables())
    )
    moment_rows, whole = pl.pallas_call(
        sync_kernel,
        out_shape=(
            jax.ShapeDtypeStruct((rows, 128), jnp.float32),
            jax.ShapeDtypeStruct((NY, 2, COLOURS, ROWS, 128), jnp.bfloat16),
        ),
        in_specs=[in_hbm] * 5,
        out_specs=(in_vmem, in_vmem),
        scratch_shapes=[
            pltpu.VMEM((rows, 128), jnp.float32),
            pltpu.VMEM((rows, 128), jnp.bfloat16),
            pltpu.VMEM((ROWS, 128), jnp.bfloat16),
            pltpu.VMEM(indices.shape[1:], jnp.int32),
            pltpu.VMEM((2, 128, 128), jnp.float32),
            pltpu.VMEM((COLOURS, 128, ROWS), jnp.float32),
            pltpu.VMEM((COLOURS, 3, TOPK, 128), jnp.float32),
            pltpu.VMEM((peers, 3, TOPK, 128), jnp.float32),
            dma((5,)), dma, dma((peers,)), dma, dma((len(ALIKE),)), dma, dma((7, NY)), dma, dma,
        ],
        compiler_params=pltpu.CompilerParams(
            collective_id=0, has_side_effects=True, vmem_limit_bytes=24 * 2**20
        ),
    )(*(pltpu.with_memory_space_constraint(operand, pltpu.HBM) for operand in operands))
    weight_out = from_rows(whole.reshape(-1, 128), layers)
    return (from_rows(moment_rows, layers)[None], weight_out)


def solution(mesh):
    return jax.shard_map(
        shards,
        mesh=mesh,
        in_specs=(
            P("dp", None, "fsdp"),
            P("dp", None, "fsdp"),
            P(None, "fsdp"),
            P("dp", None, None, "fsdp"),
        ),
        out_specs=(P("dp", None, "fsdp"), P()),
        check_vma=False,
    )
```

```python
import math

import jax
import jax.numpy as jnp
import numpy as np
from jax import lax
from jax.experimental import pallas as pl
from jax.experimental.pallas import tpu as pltpu
from jax.sharding import PartitionSpec as P

STRETCH = 64
TOPK = 4
NX, NY, NZ = 4, 8, 8
COLOURS = 8
ROWS = 128
HALF = ROWS // 2

decay_rate = 0.999
rate_step = 0.125

ALIKE = (
    (1, 1, -1), (-1, -1, 1), (-1, 2, 0), (1, -2, 0), (1, 0, 2), (0, 3, -1), (0, -3, 1), (0, 1, -3), (0, -1, 3),
    (0, 2, 2), (0, -2, -2), (1, 3, 1), (-1, -3, -1), (2, 4, 0), (1, 4, -2),
)
AROUND = ((1, 0, 0), (-1, 0, 0), (0, 1, 0), (0, -1, 0), (0, 0, 1), (0, 0, -1))
UNITS = ((0, 0),) + tuple((dy, dx % 2) for dx, dy, dz in ALIKE)
DETOUR = {(0, 1): (0, 1, 1), (1, 1): (0, -1, -1), (2, 1): (1, 0, -2), (2, 0): (-1, 0, 2), (-2, 1): (1, 0, -2), (-2, 0): (-1, 0, 2)}
ACROSS = tuple(DETOUR.get(unit, (2, 0, 0)) for unit in UNITS)


def pair_tables():
    k = np.arange(STRETCH, dtype=np.float64)[:, None]
    n = np.arange(STRETCH, dtype=np.float64)[None, :]
    scale = np.where(k == 0, math.sqrt(1.0 / STRETCH), math.sqrt(2.0 / STRETCH))
    cosine = np.kron(np.eye(2), scale * np.cos(math.pi * (2.0 * n + 1.0) * k / (2.0 * STRETCH)))

    return np.stack([cosine.T, cosine]).astype(np.float32)


def iota(shape, dim):
    return lax.broadcasted_iota(jnp.int32, shape, dim)


def lane_gather(values, lanes):
    return jnp.take_along_axis(values, lanes, axis=1, mode="promise_in_bounds")


def split(values):
    high = values.astype(jnp.bfloat16)
    low = (values - high.astype(jnp.float32)).astype(jnp.bfloat16)
    return jnp.concatenate([high, low], axis=1)


def table_dot(rows, table):
    both = jnp.dot(
        split(rows),
        jnp.concatenate([table, table], axis=0),
        preferred_element_type=jnp.float32,
    )
    return both[:, :128] + both[:, 128:]


def sync_kernel(momentum_in, gradients_in, weight_in, indices_in, tables_in, moment_out, whole,
                momentum, gradients, weight, indices, tables, kept_columns, message, inbox, loaded,
                list_sent, list_here, alike_sent, alike_here, around_sent, around_here, twin_sent, twin_here):
    dp = lax.axis_index("dp")
    fsdp = lax.axis_index("fsdp")
    z, x = lax.div(dp, NX), lax.rem(dp, NX)
    y, core = lax.div(fsdp, 2), lax.rem(fsdp, 2)
    colour = lax.rem(2 * x + y + 3 * z, COLOURS)
    odd = lax.rem(x, 2)
    parities = [odd, 1 - odd]
    xs = [lax.rem(x + d, NX) for d in range(NX)]
    ys = [lax.rem(y + d, NY) for d in range(NY)]
    zs = [lax.rem(z + d, NZ) for d in range(NZ)]
    tints = [lax.rem(colour + d, COLOURS) for d in range(COLOURS)]

    def chip(dx, dy, dz):
        return (zs[dz % NZ] * NX + xs[dx % NX], ys[dy % NY] * 2 + core)

    twin = (dp, y * 2 + 1 - core)

    own_rows = pl.ds(pl.multiple_of(colour * ROWS + odd * HALF, HALF), HALF)
    loads = [
        pltpu.make_async_copy(source, target, loaded.at[number])
        for number, (source, target) in enumerate((
            (indices_in, indices), (tables_in, tables), (momentum_in, momentum),
            (gradients_in, gradients), (weight_in.at[own_rows], weight),
        ))
    ]
    for load in loads:
        load.start()

    plane = [(dx, dz) for dz in (4, 3, 5, 2, 6, 1, 7, 0) for dx in (2, 1, 3, 0) if (dx, dz) != (0, 0)]
    barrier = pltpu.get_barrier_semaphore()
    for dx, dz in plane:
        pl.semaphore_signal(barrier, 1, device_id=chip(dx, 0, dz))
    others = sorted(step for step in set(ALIKE + AROUND + ACROSS) if step[1] != 0)
    for dx, dy, dz in others:
        pl.semaphore_signal(barrier, 1, device_id=chip(-dx, -dy, -dz))
    pl.semaphore_signal(barrier, 1, device_id=twin)

    lane = iota((8, 128), 1)
    even = iota((TOPK, 128), 1) % 2 == 0
    component = iota((STRETCH, 128), 0)
    front = iota((TOPK, 128), 1) < HALF

    for load in loads[:4]:
        load.wait()

    forward, backward = split(tables[0]), split(tables[1])

    def driven_rows(rows):
        return decay_rate * momentum[rows, :] + gradients[rows, :].astype(jnp.float32)

    def transform(share, carry):
        rows = pl.ds(pl.multiple_of(share * ROWS, ROWS), ROWS)
        columns = table_dot(driven_rows(rows), forward).T
        listed = jnp.concatenate([indices[0, :, rows], indices[1, :, rows]], axis=0)
        below = lane_gather(listed, (lane + 127) % 128)
        above = lane_gather(listed, (lane + 1) % 128)
        places = (
            jnp.where(even, listed[:TOPK], below[TOPK:]),
            jnp.where(even, above[:TOPK], listed[TOPK:]),
        )
        picked = []
        for half in range(2):
            part = columns[STRETCH * half : STRETCH * (half + 1)]
            kept = jnp.zeros((STRETCH, 128), jnp.float32)
            for slot in range(TOPK):
                match = component == places[half][slot : slot + 1]
                picked.append(jnp.sum(jnp.where(match, part, 0.0), axis=0, keepdims=True))
                kept = jnp.where(match, part, kept)
            kept_columns[share, pl.ds(STRETCH * half, STRETCH), :] = kept
        for number, rows_of in enumerate((jnp.concatenate(picked, axis=0), jnp.concatenate(places, axis=0))):
            turned = lane_gather(rows_of, (lane + HALF) % 128)
            tiles = (
                jnp.where(front, rows_of[:TOPK], turned[TOPK:]),
                jnp.where(front, turned[:TOPK], rows_of[TOPK:]),
            )
            for half in range(2):
                tile = tiles[half]
                if number == 0:
                    message[2 * share + half, 0] = tile[:2]
                    message[2 * share + half, 1] = tile[2:]
                else:
                    message[2 * share + half, 2] = (tile[:2] + 65536 * tile[2:]).astype(jnp.float32)
        return carry

    lax.fori_loop(0, COLOURS, transform, 0)

    pl.semaphore_wait(barrier, len(plane) + len(others) + 1)

    for number, (dx, dz) in enumerate(plane):
        pltpu.make_async_remote_copy(
            src_ref=message.at[2 * tints[(2 * dx + 3 * dz) % COLOURS] + parities[dx % 2]], dst_ref=inbox.at[number], send_sem=list_sent,
            recv_sem=list_here.at[number], device_id=chip(dx, 0, dz),
        ).start()

    def keep_rest(share, carry):
        rows = pl.ds(pl.multiple_of(share * ROWS, ROWS), ROWS)
        moment_out[rows, :] = driven_rows(rows) - table_dot(kept_columns[share].T, backward)
        return carry

    lax.fori_loop(0, COLOURS, keep_rest, 0)

    def list_sum(tile):
        coded = tile[2].astype(jnp.int32)
        places = (coded % 65536, coded // 65536)
        term = jnp.zeros((STRETCH, 128), jnp.float32)
        for slot in range(TOPK):
            match = component == places[slot // 2][slot % 2 : slot % 2 + 1]
            term = jnp.where(match, tile[slot // 2, pl.ds(slot % 2, 1), :], term)
        return term

    def add_list(number, summed):
        pltpu.make_async_copy(inbox.at[number], inbox.at[number], list_here.at[number]).wait()
        return summed + list_sum(inbox.at[number])

    summed = lax.fori_loop(0, len(plane), add_list, list_sum(message.at[2 * colour + odd]))
    turned = lane_gather(summed, (iota((STRETCH, 128), 1) + HALF) % 128)
    restored = table_dot(jnp.concatenate([summed, turned], axis=0).T[:HALF], backward)
    loads[4].wait()
    whole[y, core, colour, odd] = (weight[...].astype(jnp.float32) - rate_step * restored).astype(jnp.bfloat16)

    def block(plane, tint, half):
        return whole.at[plane, core, tint, half]

    def send(what, sent, here, where):
        pltpu.make_async_remote_copy(
            src_ref=what, dst_ref=what, send_sem=sent, recv_sem=here, device_id=where
        ).start()

    def pass_on(number):
        dy, parity = UNITS[number]
        what = block(ys[-dy % NY], colour, parities[parity])
        for way, step in enumerate(AROUND + (ACROSS[number],)):
            send(what, around_sent, around_here.at[way, number], chip(*step))
        send(what, twin_sent, twin_here, twin)

    def collect(number):
        dy, parity = UNITS[number]
        for way, step in enumerate(AROUND + (ACROSS[number],)):
            tint = tints[-(2 * step[0] + step[1] + 3 * step[2]) % COLOURS]
            what = block(ys[(-step[1] - dy) % NY], tint, parities[(step[0] + parity) % 2])
            pltpu.make_async_copy(what, what, around_here.at[way, number]).wait()
            send(what, twin_sent, twin_here, twin)

    for number, step in enumerate(ALIKE):
        send(block(y, colour, odd), alike_sent.at[number // 14], alike_here.at[number], chip(*step))
    pass_on(0)
    for number, step in enumerate(ALIKE):
        dy, parity = UNITS[number + 1]
        what = block(ys[-dy % NY], colour, parities[parity])
        pltpu.make_async_copy(what, what, alike_here.at[number]).wait()
        pass_on(number + 1)
    for number in range(len(UNITS)):
        collect(number)

    def await_bytes(ref, semaphore):
        pltpu.make_async_copy(ref, ref, semaphore).wait()

    await_bytes(inbox, list_sent)
    await_bytes(whole.at[0, core, pl.ds(0, 7)], alike_sent.at[0])
    await_bytes(whole.at[0, core, 7, 0], alike_sent.at[1])
    await_bytes(whole.at[pl.ds(0, 7), core], around_sent)
    await_bytes(whole.at[:, core], twin_sent)
    await_bytes(whole.at[:, 1 - core], twin_here)


def settle_kernel(moment_rows, whole, moment_out, weight_out, written):
    copies = [pltpu.make_async_copy(moment_rows, moment_out, written.at[NY])]
    for plane in range(NY):
        copies.append(pltpu.make_async_copy(whole.at[plane], weight_out.at[plane], written.at[plane]))
    for copy in copies:
        copy.start()
    for copy in copies:
        copy.wait()


def as_rows(array):
    layers, entries = array.shape
    return array.reshape(layers, entries // 128, 128).transpose(1, 0, 2).reshape(layers * entries // 128, 128)


def from_rows(array, layers):
    pieces = array.shape[0] // layers
    return array.reshape(pieces, layers, 128).transpose(1, 0, 2).reshape(layers, pieces * 128)


def shards(momentum, gradients, weight, indices):
    layers, entries = weight.shape
    rows = layers * entries // 128
    in_hbm = pl.BlockSpec(memory_space=pltpu.HBM)
    in_vmem = pl.BlockSpec(memory_space=pltpu.VMEM)
    dma = pltpu.SemaphoreType.DMA
    peers = NX * NZ - 1
    operands = (
        as_rows(momentum[0]), as_rows(gradients[0]), as_rows(weight), indices[0], jnp.asarray(pair_tables())
    )
    moment_rows, whole = pl.pallas_call(
        sync_kernel,
        out_shape=(
            jax.ShapeDtypeStruct((rows, 128), jnp.float32),
            jax.ShapeDtypeStruct((NY, 2, COLOURS, 2, HALF, 128), jnp.bfloat16),
        ),
        in_specs=[in_hbm] * 5,
        out_specs=(in_vmem, in_vmem),
        scratch_shapes=[
            pltpu.VMEM((rows, 128), jnp.float32),
            pltpu.VMEM((rows, 128), jnp.bfloat16),
            pltpu.VMEM((HALF, 128), jnp.bfloat16),
            pltpu.VMEM(indices.shape[1:], jnp.int32),
            pltpu.VMEM((2, 128, 128), jnp.float32),
            pltpu.VMEM((COLOURS, 128, ROWS), jnp.float32),
            pltpu.VMEM((2 * COLOURS, 3, 2, 128), jnp.float32),
            pltpu.VMEM((peers, 3, 2, 128), jnp.float32),
            dma((5,)), dma, dma((peers,)), dma((2,)), dma((len(ALIKE),)), dma, dma((7, len(UNITS))), dma, dma,
        ],
        compiler_params=pltpu.CompilerParams(
            collective_id=0, has_side_effects=True, vmem_limit_bytes=24 * 2**20
        ),
    )(*(pltpu.with_memory_space_constraint(operand, pltpu.HBM) for operand in operands))
    moment_rows, whole = pl.pallas_call(
        settle_kernel,
        out_shape=(
            jax.ShapeDtypeStruct(moment_rows.shape, jnp.float32),
            jax.ShapeDtypeStruct(whole.shape, jnp.bfloat16),
        ),
        in_specs=[in_vmem] * 2,
        out_specs=(in_hbm, in_hbm),
        scratch_shapes=[dma((NY + 1,))],
        compiler_params=pltpu.CompilerParams(vmem_limit_bytes=8 * 2**20),
    )(moment_rows, whole)
    weight_out = from_rows(whole.reshape(-1, 128), layers)
    return (from_rows(moment_rows, layers)[None], weight_out)


def solution(mesh):
    return jax.shard_map(
        shards,
        mesh=mesh,
        in_specs=(
            P("dp", None, "fsdp"),
            P("dp", None, "fsdp"),
            P(None, "fsdp"),
            P("dp", None, None, "fsdp"),
        ),
        out_specs=(P("dp", None, "fsdp"), P()),
        check_vma=False,
    )
```

```python
import math

import jax
import jax.numpy as jnp
import numpy as np
from jax import lax
from jax.experimental import pallas as pl
from jax.experimental.pallas import tpu as pltpu
from jax.sharding import PartitionSpec as P

STRETCH = 64
TOPK = 4
NX, NY, NZ = 4, 8, 8
COLOURS = 8
ROWS = 128
HALF = ROWS // 2

decay_rate = 0.999
rate_step = 0.125

STEPS = (
    (0, -1, 0, 0), (0, 1, 0, 0), (0, 0, 0, -1), (0, -1, 1, 0), (0, 0, 0, 2), (0, 0, -2, 0), (0, 1, 0, -1),
    (0, 0, 2, 0), (0, 0, 0, -2), (0, 0, 0, 1), (0, -1, -1, 0), (0, 0, -3, 1), (1, 0, 0, -1), (0, 2, 2, 0),
    (2, 0, 0, 1), (3, 0, -1, 0), (4, 1, 0, 0), (4, 0, 0, 1), (0, -1, 4, 0), (0, -1, 0, -2), (6, 0, 0, -1),
    (8, 0, 0, 1), (6, 1, 0, 0), (4, -1, 0, -1), (2, 1, 0, 0), (7, 1, 0, 0), (4, 0, 2, 0), (2, 0, 2, -1),
    (8, 1, 0, 0), (11, -1, 0, 0), (4, -1, 0, 0), (5, 0, -3, 0), (11, 0, 0, 1), (9, 1, 0, 0), (6, 0, -1, -2),
    (11, 0, 0, 2), (11, 0, -1, 0), (12, 0, 0, -1), (12, -1, 0, 0), (12, 0, 1, 0), (6, 1, -1, -1), (5, 0, 1, 0),
    (4, 2, 0, 0), (16, -1, 0, 0), (16, 1, 0, 0), (14, 0, 0, 1), (6, 0, 1, 0), (15, 0, 1, 0), (15, 0, -1, 0),
    (8, 0, 1, 0), (9, 0, -1, 0), (12, 1, -1, 0), (17, 0, 0, -1), (14, 0, 0, 2), (19, -1, 0, 0), (19, 0, 0, -1),
    (12, 0, -2, 0), (18, 0, -1, 0), (19, 0, 0, 1), (8, 1, 1, -1), (21, 0, 0, -1), (26, 0, -1, 0), (13, 0, 1, 0),
    (14, 0, 0, -1), (27, 0, 0, -1), (18, -1, 0, 0), (28, 0, 0, -1), (17, 0, 0, 1), (23, 0, 1, 0), (19, 1, 0, 0),
    (21, -1, 0, 0), (22, -1, 0, 0), (23, 1, 0, 0), (27, 0, 0, 1), (27, -1, 0, 0), (27, 0, -1, 0), (30, 0, 0, 1),
    (29, 0, 1, 0), (24, 1, 1, 0), (28, -1, 0, 0), (28, 0, -1, 0), (32, 0, 0, 1), (32, 1, 0, 0), (35, 0, 0, -1),
    (24, 0, 2, 0), (33, 1, 0, 0), (34, 0, 1, 0), (32, 0, -1, 0), (41, -1, 0, 0), (39, 0, 0, 1), (36, 1, 0, 0),
    (39, 0, 1, 0), (44, 0, 0, -1), (35, 0, -1, 0), (38, 1, 0, 0), (46, 0, 1, 0), (35, -1, 0, 1), (30, 0, -1, 1),
    (36, 0, -1, 0), (46, -1, 0, 0), (40, 0, 0, 1), (52, 1, 0, 0), (52, 0, 0, -1), (52, 0, 1, 0), (37, 0, -1, 0),
    (54, -1, 0, 0), (48, 0, 0, 1), (53, 0, 0, -1), (54, 0, 1, 0), (56, 1, 0, 0), (45, 0, -1, 0), (58, -1, 0, 0),
    (52, 0, 0, 1), (55, 0, 0, -1), (55, 0, 1, 0), (57, 1, 0, 0), (49, 0, -1, 0), (61, -1, 0, 0), (57, 0, 0, 1),
    (60, 0, 0, -1), (57, 0, 1, 0), (65, 1, 0, 0), (62, 0, -1, 0), (59, 0, 0, 1), (65, 0, 0, -1), (60, 0, 1, 0),
    (67, 1, 0, 0),
)
SENDS = (
    4, 6, 1, 8, 2, 5, 3, 7, 12, 9, 10, 19, 11, 20, 14, 13, 25, 28, 15, 16, 24, 31, 17, 27, 43, 18, 32, 42, 21, 47,
    35, 23, 41, 26, 50, 22, 60, 29, 51, 34, 36, 30, 33, 37, 38, 40, 39, 52, 57, 63, 64, 54, 46, 48, 49, 44, 45, 53,
    68, 66, 58, 55, 59, 56, 70, 61, 71, 72, 69, 73, 79, 85, 62, 65, 75, 74, 76, 67, 81, 80, 78, 98, 77, 82, 88, 83,
    86, 87, 94, 97, 84, 91, 99, 105, 95, 90, 92, 101, 89, 93, 111, 100, 96, 107, 117, 113, 102, 103, 104, 108, 106,
    109, 114, 115, 110, 119, 116, 121, 112, 124, 126, 120, 118, 123, 122, 125, 127,
)


def total_steps():
    ways = [(0, 0, 0)]
    for source, *jump in STEPS:
        ways.append(tuple(a + b for a, b in zip(ways[source], jump)))
    after = [[] for way in ways]
    for number in SENDS:
        source, *jump = STEPS[number - 1]
        after[source].append((number, tuple(jump)))
    return ways, after


def pair_tables():
    k = np.arange(STRETCH, dtype=np.float64)[:, None]
    n = np.arange(STRETCH, dtype=np.float64)[None, :]
    scale = np.where(k == 0, math.sqrt(1.0 / STRETCH), math.sqrt(2.0 / STRETCH))
    cosine = np.kron(np.eye(2), scale * np.cos(math.pi * (2.0 * n + 1.0) * k / (2.0 * STRETCH)))

    return np.stack([cosine.T, cosine]).astype(np.float32)


def iota(shape, dim):
    return lax.broadcasted_iota(jnp.int32, shape, dim)


def lane_gather(values, lanes):
    return jnp.take_along_axis(values, lanes, axis=1, mode="promise_in_bounds")


def split(values):
    high = values.astype(jnp.bfloat16)
    low = (values - high.astype(jnp.float32)).astype(jnp.bfloat16)
    return jnp.concatenate([high, low], axis=1)


def table_dot(rows, table):
    both = jnp.dot(
        split(rows),
        jnp.concatenate([table, table], axis=0),
        preferred_element_type=jnp.float32,
    )
    return both[:, :128] + both[:, 128:]


def sync_kernel(momentum_in, gradients_in, weight_in, indices_in, tables_in, moment_out, whole,
                momentum, gradients, weight, indices, tables, kept_columns, message, inbox, loaded,
                list_sent, list_here, passed_on, here, twin_sent, twin_here):
    dp = lax.axis_index("dp")
    fsdp = lax.axis_index("fsdp")
    z, x = lax.div(dp, NX), lax.rem(dp, NX)
    y, core = lax.div(fsdp, 2), lax.rem(fsdp, 2)
    colour = lax.rem(2 * x + y + 3 * z, COLOURS)
    odd = lax.rem(x, 2)
    parities = [odd, 1 - odd]
    xs = [lax.rem(x + d, NX) for d in range(NX)]
    ys = [lax.rem(y + d, NY) for d in range(NY)]
    zs = [lax.rem(z + d, NZ) for d in range(NZ)]
    tints = [lax.rem(colour + d, COLOURS) for d in range(COLOURS)]

    def chip(dx, dy, dz):
        return (zs[dz % NZ] * NX + xs[dx % NX], ys[dy % NY] * 2 + core)

    twin = (dp, y * 2 + 1 - core)

    own_rows = pl.ds(pl.multiple_of(colour * ROWS + odd * HALF, HALF), HALF)
    loads = [
        pltpu.make_async_copy(source, target, loaded.at[number])
        for number, (source, target) in enumerate((
            (indices_in, indices), (tables_in, tables), (momentum_in, momentum),
            (gradients_in, gradients), (weight_in.at[own_rows], weight),
        ))
    ]
    for load in loads:
        load.start()

    plane = [(dx, dz) for dz in (0, 1, 7, 2, 6, 3, 5, 4) for dx in (0, 1, 3, 2) if (dx, dz) != (0, 0)]
    barrier = pltpu.get_barrier_semaphore()
    for dx, dz in reversed(plane):
        pl.semaphore_signal(barrier, 1, device_id=chip(dx, 0, dz))
    ways, after = total_steps()
    others = sorted({(dx % NX, dy % NY, dz % NZ) for source, dx, dy, dz in STEPS if dy != 0})
    for dx, dy, dz in others:
        pl.semaphore_signal(barrier, 1, device_id=chip(-dx, -dy, -dz))
    pl.semaphore_signal(barrier, 1, device_id=twin)

    lane = iota((8, 128), 1)
    even = iota((TOPK, 128), 1) % 2 == 0
    component = iota((STRETCH, 128), 0)
    front = iota((TOPK, 128), 1) < HALF

    for load in loads[:4]:
        load.wait()

    forward, backward = split(tables[0]), split(tables[1])

    def driven_rows(rows):
        return decay_rate * momentum[rows, :] + gradients[rows, :].astype(jnp.float32)

    def transform(share, carry):
        rows = pl.ds(pl.multiple_of(share * ROWS, ROWS), ROWS)
        columns = table_dot(driven_rows(rows), forward).T
        listed = jnp.concatenate([indices[0, :, rows], indices[1, :, rows]], axis=0)
        below = lane_gather(listed, (lane + 127) % 128)
        above = lane_gather(listed, (lane + 1) % 128)
        places = (
            jnp.where(even, listed[:TOPK], below[TOPK:]),
            jnp.where(even, above[:TOPK], listed[TOPK:]),
        )
        picked = []
        for half in range(2):
            part = columns[STRETCH * half : STRETCH * (half + 1)]
            kept = jnp.zeros((STRETCH, 128), jnp.float32)
            for slot in range(TOPK):
                match = component == places[half][slot : slot + 1]
                picked.append(jnp.sum(jnp.where(match, part, 0.0), axis=0, keepdims=True))
                kept = jnp.where(match, part, kept)
            kept_columns[share, pl.ds(STRETCH * half, STRETCH), :] = kept
        for number, rows_of in enumerate((jnp.concatenate(picked, axis=0), jnp.concatenate(places, axis=0))):
            turned = lane_gather(rows_of, (lane + HALF) % 128)
            tiles = (
                jnp.where(front, rows_of[:TOPK], turned[TOPK:]),
                jnp.where(front, turned[:TOPK], rows_of[TOPK:]),
            )
            for half in range(2):
                tile = tiles[half]
                if number == 0:
                    message[2 * share + half, 0] = tile[:2]
                    message[2 * share + half, 1] = tile[2:]
                else:
                    message[2 * share + half, 2] = (tile[:2] + 65536 * tile[2:]).astype(jnp.float32)
        return carry

    lax.fori_loop(0, COLOURS, transform, 0, unroll=4)

    pl.semaphore_wait(barrier, len(plane) + len(others) + 1)

    for number, (dx, dz) in reversed(list(enumerate(plane))):
        pltpu.make_async_remote_copy(
            src_ref=message.at[2 * tints[(2 * dx + 3 * dz) % COLOURS] + parities[dx % 2]], dst_ref=inbox.at[number], send_sem=list_sent,
            recv_sem=list_here.at[number], device_id=chip(dx, 0, dz),
        ).start()

    def keep_rest(share, carry):
        rows = pl.ds(pl.multiple_of(share * ROWS, ROWS), ROWS)
        moment_out[rows, :] = driven_rows(rows) - table_dot(kept_columns[share].T, backward)
        return carry

    lax.fori_loop(0, COLOURS, keep_rest, 0)

    def list_sum(tile):
        coded = tile[2].astype(jnp.int32)
        places = (coded % 65536, coded // 65536)
        term = jnp.zeros((STRETCH, 128), jnp.float32)
        for slot in range(TOPK):
            match = component == places[slot // 2][slot % 2 : slot % 2 + 1]
            term = jnp.where(match, tile[slot // 2, pl.ds(slot % 2, 1), :], term)
        return term

    def add_list(number, summed):
        pltpu.make_async_copy(inbox.at[number], inbox.at[number], list_here.at[number]).wait()
        return summed + list_sum(inbox.at[number])

    summed = lax.fori_loop(0, len(plane), add_list, list_sum(message.at[2 * colour + odd]))
    turned = lane_gather(summed, (iota((STRETCH, 128), 1) + HALF) % 128)
    restored = table_dot(jnp.concatenate([summed, turned], axis=0).T[:HALF], backward)
    loads[4].wait()
    whole[y, core, colour, odd] = (weight[...].astype(jnp.float32) - rate_step * restored).astype(jnp.bfloat16)

    def block(plane, tint, half):
        return whole.at[plane, core, tint, half]

    def send(what, sent, here, where):
        pltpu.make_async_remote_copy(
            src_ref=what, dst_ref=what, send_sem=sent, recv_sem=here, device_id=where
        ).start()

    def have(number):
        dx, dy, dz = ways[number]
        what = block(ys[-dy % NY], tints[-(2 * dx + dy + 3 * dz) % COLOURS], parities[dx % 2])
        if number > 0:
            pltpu.make_async_copy(what, what, here.at[number]).wait()
        for follower, step in after[number]:
            send(what, passed_on.at[(sent[0] >= 112) + (sent[0] >= 126)], here.at[follower], chip(*step))
            sent[0] += 1
        send(what, twin_sent, twin_here, twin)

    sent = [0]
    for number in range(len(ways)):
        have(number)

    def await_bytes(ref, semaphore):
        pltpu.make_async_copy(ref, ref, semaphore).wait()

    await_bytes(inbox, list_sent)
    await_bytes(whole.at[pl.ds(0, 7), core], passed_on.at[0])
    await_bytes(whole.at[0, core, pl.ds(0, 7)], passed_on.at[1])
    await_bytes(whole.at[0, core, 7, 0], passed_on.at[2])
    await_bytes(whole.at[:, core], twin_sent)
    await_bytes(whole.at[:, 1 - core], twin_here)


def settle_kernel(moment_rows, whole, moment_out, weight_out, written):
    copies = [pltpu.make_async_copy(moment_rows, moment_out, written.at[NY])]
    for plane in range(NY):
        copies.append(pltpu.make_async_copy(whole.at[plane], weight_out.at[plane], written.at[plane]))
    for copy in copies:
        copy.start()
    for copy in copies:
        copy.wait()


def as_rows(array):
    layers, entries = array.shape
    return array.reshape(layers, entries // 128, 128).transpose(1, 0, 2).reshape(layers * entries // 128, 128)


def from_rows(array, layers):
    pieces = array.shape[0] // layers
    return array.reshape(pieces, layers, 128).transpose(1, 0, 2).reshape(layers, pieces * 128)


def shards(momentum, gradients, weight, indices):
    layers, entries = weight.shape
    rows = layers * entries // 128
    in_hbm = pl.BlockSpec(memory_space=pltpu.HBM)
    in_vmem = pl.BlockSpec(memory_space=pltpu.VMEM)
    dma = pltpu.SemaphoreType.DMA
    peers = NX * NZ - 1
    operands = (
        as_rows(momentum[0]), as_rows(gradients[0]), as_rows(weight), indices[0], jnp.asarray(pair_tables())
    )
    moment_rows, whole = pl.pallas_call(
        sync_kernel,
        out_shape=(
            jax.ShapeDtypeStruct((rows, 128), jnp.float32),
            jax.ShapeDtypeStruct((NY, 2, COLOURS, 2, HALF, 128), jnp.bfloat16),
        ),
        in_specs=[in_hbm] * 5,
        out_specs=(in_vmem, in_vmem),
        scratch_shapes=[
            pltpu.VMEM((rows, 128), jnp.float32),
            pltpu.VMEM((rows, 128), jnp.bfloat16),
            pltpu.VMEM((HALF, 128), jnp.bfloat16),
            pltpu.VMEM(indices.shape[1:], jnp.int32),
            pltpu.VMEM((2, 128, 128), jnp.float32),
            pltpu.VMEM((COLOURS, 128, ROWS), jnp.float32),
            pltpu.VMEM((2 * COLOURS, 3, 2, 128), jnp.float32),
            pltpu.VMEM((peers, 3, 2, 128), jnp.float32),
            dma((5,)), dma, dma((peers,)), dma((3,)), dma((len(STEPS) + 1,)), dma, dma,
        ],
        compiler_params=pltpu.CompilerParams(
            collective_id=0, has_side_effects=True, vmem_limit_bytes=24 * 2**20
        ),
    )(*(pltpu.with_memory_space_constraint(operand, pltpu.HBM) for operand in operands))
    moment_rows, whole = pl.pallas_call(
        settle_kernel,
        out_shape=(
            jax.ShapeDtypeStruct(moment_rows.shape, jnp.float32),
            jax.ShapeDtypeStruct(whole.shape, jnp.bfloat16),
        ),
        in_specs=[in_vmem] * 2,
        out_specs=(in_hbm, in_hbm),
        scratch_shapes=[dma((NY + 1,))],
        compiler_params=pltpu.CompilerParams(vmem_limit_bytes=8 * 2**20),
    )(moment_rows, whole)
    weight_out = from_rows(whole.reshape(-1, 128), layers)
    return (from_rows(moment_rows, layers)[None], weight_out)


def solution(mesh):
    return jax.shard_map(
        shards,
        mesh=mesh,
        in_specs=(
            P("dp", None, "fsdp"),
            P("dp", None, "fsdp"),
            P(None, "fsdp"),
            P("dp", None, None, "fsdp"),
        ),
        out_specs=(P("dp", None, "fsdp"), P()),
        check_vma=False,
    )
```

```python
import math

import jax
import jax.numpy as jnp
import numpy as np
from jax import lax
from jax.experimental import pallas as pl
from jax.experimental.pallas import tpu as pltpu
from jax.sharding import PartitionSpec as P

STRETCH = 64
TOPK = 4
NX, NY, NZ = 4, 8, 8
COLOURS = 8
ROWS = 128
HALF = ROWS // 2

decay_rate = 0.999
rate_step = 0.125

STEPS = (
    (0, -1, 0, 0), (0, 1, 0, 0), (0, 0, 0, -1), (0, -1, 1, 0), (0, 0, 0, 2), (0, 0, -2, 0), (0, 1, 0, -1),
    (0, 0, 2, 0), (0, 0, 0, -2), (0, 0, 0, 1), (0, -1, -1, 0), (0, 0, -3, 1), (1, 0, 0, -1), (0, 2, 2, 0),
    (2, 0, 0, 1), (3, 0, -1, 0), (4, 1, 0, 0), (4, 0, 0, 1), (0, -1, 4, 0), (0, -1, 0, -2), (6, 0, 0, -1),
    (8, 0, 0, 1), (6, 1, 0, 0), (4, -1, 0, -1), (2, 1, 0, 0), (7, 1, 0, 0), (4, 0, 2, 0), (2, 0, 2, -1),
    (8, 1, 0, 0), (11, -1, 0, 0), (4, -1, 0, 0), (5, 0, -3, 0), (11, 0, 0, 1), (9, 1, 0, 0), (6, 0, -1, -2),
    (11, 0, 0, 2), (11, 0, -1, 0), (12, 0, 0, -1), (12, -1, 0, 0), (12, 0, 1, 0), (6, 1, -1, -1), (5, 0, 1, 0),
    (4, 2, 0, 0), (16, -1, 0, 0), (16, 1, 0, 0), (14, 0, 0, 1), (6, 0, 1, 0), (15, 0, 1, 0), (15, 0, -1, 0),
    (8, 0, 1, 0), (9, 0, -1, 0), (12, 1, -1, 0), (17, 0, 0, -1), (14, 0, 0, 2), (19, -1, 0, 0), (19, 0, 0, -1),
    (12, 0, -2, 0), (18, 0, -1, 0), (19, 0, 0, 1), (8, 1, 1, -1), (21, 0, 0, -1), (26, 0, -1, 0), (13, 0, 1, 0),
    (14, 0, 0, -1), (27, 0, 0, -1), (18, -1, 0, 0), (28, 0, 0, -1), (17, 0, 0, 1), (23, 0, 1, 0), (19, 1, 0, 0),
    (21, -1, 0, 0), (22, -1, 0, 0), (23, 1, 0, 0), (27, 0, 0, 1), (27, -1, 0, 0), (27, 0, -1, 0), (30, 0, 0, 1),
    (29, 0, 1, 0), (24, 1, 1, 0), (28, -1, 0, 0), (28, 0, -1, 0), (32, 0, 0, 1), (32, 1, 0, 0), (35, 0, 0, -1),
    (24, 0, 2, 0), (33, 1, 0, 0), (34, 0, 1, 0), (32, 0, -1, 0), (41, -1, 0, 0), (39, 0, 0, 1), (36, 1, 0, 0),
    (39, 0, 1, 0), (44, 0, 0, -1), (35, 0, -1, 0), (38, 1, 0, 0), (46, 0, 1, 0), (35, -1, 0, 1), (30, 0, -1, 1),
    (36, 0, -1, 0), (46, -1, 0, 0), (40, 0, 0, 1), (52, 1, 0, 0), (52, 0, 0, -1), (52, 0, 1, 0), (37, 0, -1, 0),
    (54, -1, 0, 0), (48, 0, 0, 1), (53, 0, 0, -1), (54, 0, 1, 0), (56, 1, 0, 0), (45, 0, -1, 0), (58, -1, 0, 0),
    (52, 0, 0, 1), (55, 0, 0, -1), (55, 0, 1, 0), (57, 1, 0, 0), (49, 0, -1, 0), (61, -1, 0, 0), (57, 0, 0, 1),
    (60, 0, 0, -1), (57, 0, 1, 0), (65, 1, 0, 0), (62, 0, -1, 0), (59, 0, 0, 1), (65, 0, 0, -1), (60, 0, 1, 0),
    (67, 1, 0, 0),
)
SENDS = (
    4, 6, 1, 8, 2, 5, 3, 7, 12, 9, 10, 19, 11, 20, 14, 13, 25, 28, 15, 16, 24, 31, 17, 27, 43, 18, 32, 42, 21, 47,
    35, 23, 41, 26, 50, 22, 60, 29, 51, 34, 36, 30, 33, 37, 38, 40, 39, 52, 57, 63, 64, 54, 46, 48, 49, 44, 45, 53,
    68, 66, 58, 55, 59, 56, 70, 61, 71, 72, 69, 73, 79, 85, 62, 65, 75, 74, 76, 67, 81, 80, 78, 98, 77, 82, 88, 83,
    86, 87, 94, 97, 84, 91, 99, 105, 95, 90, 92, 101, 89, 93, 111, 100, 96, 107, 117, 113, 102, 103, 104, 108, 106,
    109, 114, 115, 110, 119, 116, 121, 112, 124, 126, 120, 118, 123, 122, 125, 127,
)


def total_steps():
    ways = [(0, 0, 0)]
    for source, *jump in STEPS:
        ways.append(tuple(a + b for a, b in zip(ways[source], jump)))
    after = [[] for way in ways]
    for number in SENDS:
        source, *jump = STEPS[number - 1]
        after[source].append((number, tuple(jump)))
    return ways, after


def pair_tables():
    k = np.arange(STRETCH, dtype=np.float64)[:, None]
    n = np.arange(STRETCH, dtype=np.float64)[None, :]
    scale = np.where(k == 0, math.sqrt(1.0 / STRETCH), math.sqrt(2.0 / STRETCH))
    cosine = np.kron(np.eye(2), scale * np.cos(math.pi * (2.0 * n + 1.0) * k / (2.0 * STRETCH)))

    return np.stack([cosine.T, cosine]).astype(np.float32)


def iota(shape, dim):
    return lax.broadcasted_iota(jnp.int32, shape, dim)


def lane_gather(values, lanes):
    return jnp.take_along_axis(values, lanes, axis=1, mode="promise_in_bounds")


def split(values):
    high = values.astype(jnp.bfloat16)
    low = (values - high.astype(jnp.float32)).astype(jnp.bfloat16)
    return jnp.concatenate([high, low], axis=1)


def table_dot(rows, table):
    both = jnp.dot(
        split(rows),
        jnp.concatenate([table, table], axis=0),
        preferred_element_type=jnp.float32,
    )
    return both[:, :128] + both[:, 128:]


def sync_kernel(momentum_in, gradients_in, weight_in, indices_in, tables_in, moment_out, whole,
                momentum, gradients, weight, indices, tables, kept_columns, message, inbox, loaded,
                list_sent, list_here, passed_on, here, twin_sent, twin_here):
    dp = lax.axis_index("dp")
    fsdp = lax.axis_index("fsdp")
    z, x = lax.div(dp, NX), lax.rem(dp, NX)
    y, core = lax.div(fsdp, 2), lax.rem(fsdp, 2)
    colour = lax.rem(2 * x + y + 3 * z, COLOURS)
    odd = lax.rem(x, 2)
    parities = [odd, 1 - odd]
    xs = [lax.rem(x + d, NX) for d in range(NX)]
    ys = [lax.rem(y + d, NY) for d in range(NY)]
    zs = [lax.rem(z + d, NZ) for d in range(NZ)]
    tints = [lax.rem(colour + d, COLOURS) for d in range(COLOURS)]

    def chip(dx, dy, dz):
        return (zs[dz % NZ] * NX + xs[dx % NX], ys[dy % NY] * 2 + core)

    twin = (dp, y * 2 + 1 - core)

    own_rows = pl.ds(pl.multiple_of(colour * ROWS + odd * HALF, HALF), HALF)
    loads = [
        pltpu.make_async_copy(source, target, loaded.at[number])
        for number, (source, target) in enumerate((
            (indices_in, indices), (tables_in, tables), (momentum_in, momentum),
            (gradients_in, gradients), (weight_in.at[own_rows], weight),
        ))
    ]
    for load in loads:
        load.start()

    plane = [(dx, dz) for dz in (0, 1, 7, 2, 6, 3, 5, 4) for dx in (0, 1, 3, 2) if (dx, dz) != (0, 0)]
    barrier = pltpu.get_barrier_semaphore()
    ways, after = total_steps()
    others = sorted({(dx % NX, dy % NY, dz % NZ) for source, dx, dy, dz in STEPS if dy != 0})
    senders = [(-dx, -dy, -dz) for dx, dy, dz in others] + [(dx, 0, dz) for dx, dz in plane]
    senders.sort(key=lambda step: -sum(min(d % n, -d % n) for d, n in zip(step, (NX, NY, NZ))))
    for step in senders:
        pl.semaphore_signal(barrier, 1, device_id=chip(*step))
    pl.semaphore_signal(barrier, 1, device_id=twin)

    lane = iota((8, 128), 1)
    even = iota((TOPK, 128), 1) % 2 == 0
    component = iota((STRETCH, 128), 0)
    front = iota((TOPK, 128), 1) < HALF

    for load in loads[:4]:
        load.wait()

    forward, backward = split(tables[0]), split(tables[1])

    def driven_rows(rows):
        return decay_rate * momentum[rows, :] + gradients[rows, :].astype(jnp.float32)

    def transform(share, carry):
        rows = pl.ds(pl.multiple_of(share * ROWS, ROWS), ROWS)
        columns = table_dot(driven_rows(rows), forward).T
        listed = jnp.concatenate([indices[0, :, rows], indices[1, :, rows]], axis=0)
        below = lane_gather(listed, (lane + 127) % 128)
        above = lane_gather(listed, (lane + 1) % 128)
        places = (
            jnp.where(even, listed[:TOPK], below[TOPK:]),
            jnp.where(even, above[:TOPK], listed[TOPK:]),
        )
        picked = []
        for half in range(2):
            part = columns[STRETCH * half : STRETCH * (half + 1)]
            kept = jnp.zeros((STRETCH, 128), jnp.float32)
            for slot in range(TOPK):
                match = component == places[half][slot : slot + 1]
                picked.append(jnp.sum(jnp.where(match, part, 0.0), axis=0, keepdims=True))
                kept = jnp.where(match, part, kept)
            kept_columns[share, pl.ds(STRETCH * half, STRETCH), :] = kept
        for number, rows_of in enumerate((jnp.concatenate(picked, axis=0), jnp.concatenate(places, axis=0))):
            turned = lane_gather(rows_of, (lane + HALF) % 128)
            tiles = (
                jnp.where(front, rows_of[:TOPK], turned[TOPK:]),
                jnp.where(front, turned[:TOPK], rows_of[TOPK:]),
            )
            for half in range(2):
                tile = tiles[half]
                if number == 0:
                    message[2 * share + half, 0] = tile[:2]
                    message[2 * share + half, 1] = tile[2:]
                else:
                    message[2 * share + half, 2] = (tile[:2] + 65536 * tile[2:]).astype(jnp.float32)
        return carry

    lax.fori_loop(0, COLOURS, transform, 0, unroll=4)

    pl.semaphore_wait(barrier, len(plane) + len(others) + 1)

    for number, (dx, dz) in reversed(list(enumerate(plane))):
        pltpu.make_async_remote_copy(
            src_ref=message.at[2 * tints[(2 * dx + 3 * dz) % COLOURS] + parities[dx % 2]], dst_ref=inbox.at[number], send_sem=list_sent,
            recv_sem=list_here.at[number], device_id=chip(dx, 0, dz),
        ).start()

    def keep_rest(share, carry):
        rows = pl.ds(pl.multiple_of(share * ROWS, ROWS), ROWS)
        moment_out[rows, :] = driven_rows(rows) - table_dot(kept_columns[share].T, backward)
        return carry

    lax.fori_loop(0, COLOURS, keep_rest, 0)

    def list_sum(tile):
        coded = tile[2].astype(jnp.int32)
        places = (coded % 65536, coded // 65536)
        term = jnp.zeros((STRETCH, 128), jnp.float32)
        for slot in range(TOPK):
            match = component == places[slot // 2][slot % 2 : slot % 2 + 1]
            term = jnp.where(match, tile[slot // 2, pl.ds(slot % 2, 1), :], term)
        return term

    def add_list(number, summed):
        pltpu.make_async_copy(inbox.at[number], inbox.at[number], list_here.at[number]).wait()
        return summed + list_sum(inbox.at[number])

    summed = lax.fori_loop(0, len(plane), add_list, list_sum(message.at[2 * colour + odd]))
    turned = lane_gather(summed, (iota((STRETCH, 128), 1) + HALF) % 128)
    restored = table_dot(jnp.concatenate([summed, turned], axis=0).T[:HALF], backward)
    loads[4].wait()
    whole[y, core, colour, odd] = (weight[...].astype(jnp.float32) - rate_step * restored).astype(jnp.bfloat16)

    def block(plane, tint, half):
        return whole.at[plane, core, tint, half]

    def send(what, sent, here, where):
        pltpu.make_async_remote_copy(
            src_ref=what, dst_ref=what, send_sem=sent, recv_sem=here, device_id=where
        ).start()

    def have(number):
        dx, dy, dz = ways[number]
        what = block(ys[-dy % NY], tints[-(2 * dx + dy + 3 * dz) % COLOURS], parities[dx % 2])
        if number > 0:
            pltpu.make_async_copy(what, what, here.at[number]).wait()
        for follower, step in after[number]:
            send(what, passed_on.at[(sent[0] >= 112) + (sent[0] >= 126)], here.at[follower], chip(*step))
            sent[0] += 1
        send(what, twin_sent, twin_here, twin)

    sent = [0]
    for number in range(len(ways)):
        have(number)

    def await_bytes(ref, semaphore):
        pltpu.make_async_copy(ref, ref, semaphore).wait()

    await_bytes(inbox, list_sent)
    await_bytes(whole.at[pl.ds(0, 7), core], passed_on.at[0])
    await_bytes(whole.at[0, core, pl.ds(0, 7)], passed_on.at[1])
    await_bytes(whole.at[0, core, 7, 0], passed_on.at[2])
    await_bytes(whole.at[:, core], twin_sent)
    await_bytes(whole.at[:, 1 - core], twin_here)


def settle_kernel(moment_rows, whole, moment_out, weight_out, written):
    copies = [pltpu.make_async_copy(moment_rows, moment_out, written.at[NY])]
    for plane in range(NY):
        copies.append(pltpu.make_async_copy(whole.at[plane], weight_out.at[plane], written.at[plane]))
    for copy in copies:
        copy.start()
    for copy in copies:
        copy.wait()


def as_rows(array):
    layers, entries = array.shape
    return array.reshape(layers, entries // 128, 128).transpose(1, 0, 2).reshape(layers * entries // 128, 128)


def from_rows(array, layers):
    pieces = array.shape[0] // layers
    return array.reshape(pieces, layers, 128).transpose(1, 0, 2).reshape(layers, pieces * 128)


def shards(momentum, gradients, weight, indices):
    layers, entries = weight.shape
    rows = layers * entries // 128
    in_hbm = pl.BlockSpec(memory_space=pltpu.HBM)
    in_vmem = pl.BlockSpec(memory_space=pltpu.VMEM)
    dma = pltpu.SemaphoreType.DMA
    peers = NX * NZ - 1
    operands = (
        as_rows(momentum[0]), as_rows(gradients[0]), as_rows(weight), indices[0], jnp.asarray(pair_tables())
    )
    moment_rows, whole = pl.pallas_call(
        sync_kernel,
        out_shape=(
            jax.ShapeDtypeStruct((rows, 128), jnp.float32),
            jax.ShapeDtypeStruct((NY, 2, COLOURS, 2, HALF, 128), jnp.bfloat16),
        ),
        in_specs=[in_hbm] * 5,
        out_specs=(in_vmem, in_vmem),
        scratch_shapes=[
            pltpu.VMEM((rows, 128), jnp.float32),
            pltpu.VMEM((rows, 128), jnp.bfloat16),
            pltpu.VMEM((HALF, 128), jnp.bfloat16),
            pltpu.VMEM(indices.shape[1:], jnp.int32),
            pltpu.VMEM((2, 128, 128), jnp.float32),
            pltpu.VMEM((COLOURS, 128, ROWS), jnp.float32),
            pltpu.VMEM((2 * COLOURS, 3, 2, 128), jnp.float32),
            pltpu.VMEM((peers, 3, 2, 128), jnp.float32),
            dma((5,)), dma, dma((peers,)), dma((3,)), dma((len(STEPS) + 1,)), dma, dma,
        ],
        compiler_params=pltpu.CompilerParams(
            collective_id=0, has_side_effects=True, vmem_limit_bytes=24 * 2**20
        ),
    )(*(pltpu.with_memory_space_constraint(operand, pltpu.HBM) for operand in operands))
    moment_rows, whole = pl.pallas_call(
        settle_kernel,
        out_shape=(
            jax.ShapeDtypeStruct(moment_rows.shape, jnp.float32),
            jax.ShapeDtypeStruct(whole.shape, jnp.bfloat16),
        ),
        in_specs=[in_vmem] * 2,
        out_specs=(in_hbm, in_hbm),
        scratch_shapes=[dma((NY + 1,))],
        compiler_params=pltpu.CompilerParams(vmem_limit_bytes=8 * 2**20),
    )(moment_rows, whole)
    weight_out = from_rows(whole.reshape(-1, 128), layers)
    return (from_rows(moment_rows, layers)[None], weight_out)


def solution(mesh):
    return jax.shard_map(
        shards,
        mesh=mesh,
        in_specs=(
            P("dp", None, "fsdp"),
            P("dp", None, "fsdp"),
            P(None, "fsdp"),
            P("dp", None, None, "fsdp"),
        ),
        out_specs=(P("dp", None, "fsdp"), P()),
        check_vma=False,
    )
```

```python
import math

import jax
import jax.numpy as jnp
import numpy as np
from jax import lax
from jax.experimental import pallas as pl
from jax.experimental.pallas import tpu as pltpu
from jax.sharding import PartitionSpec as P

STRETCH = 64
TOPK = 4
NX, NY, NZ = 4, 8, 8
COLOURS = 8
ROWS = 128
HALF = ROWS // 2

decay_rate = 0.999
rate_step = 0.125

STEPS = (
    (0, -1, 0, 0), (0, 1, 0, 0), (0, 0, 0, -1), (0, -1, 1, 0), (0, 0, 0, 2), (0, 0, -2, 0), (0, 1, 0, -1),
    (0, 0, 2, 0), (0, 0, 0, -2), (0, 0, 0, 1), (0, -1, -1, 0), (0, 0, -3, 1), (1, 0, 0, -1), (0, 2, 2, 0),
    (2, 0, 0, 1), (3, 0, -1, 0), (4, 1, 0, 0), (4, 0, 0, 1), (0, -1, 4, 0), (0, -1, 0, -2), (6, 0, 0, -1),
    (8, 0, 0, 1), (6, 1, 0, 0), (4, -1, 0, -1), (2, 1, 0, 0), (7, 1, 0, 0), (4, 0, 2, 0), (2, 0, 2, -1),
    (8, 1, 0, 0), (11, -1, 0, 0), (4, -1, 0, 0), (5, 0, -3, 0), (11, 0, 0, 1), (9, 1, 0, 0), (6, 0, -1, -2),
    (11, 0, 0, 2), (11, 0, -1, 0), (12, 0, 0, -1), (12, -1, 0, 0), (12, 0, 1, 0), (6, 1, -1, -1), (5, 0, 1, 0),
    (4, 2, 0, 0), (16, -1, 0, 0), (16, 1, 0, 0), (14, 0, 0, 1), (6, 0, 1, 0), (15, 0, 1, 0), (15, 0, -1, 0),
    (8, 0, 1, 0), (9, 0, -1, 0), (12, 1, -1, 0), (17, 0, 0, -1), (14, 0, 0, 2), (19, -1, 0, 0), (19, 0, 0, -1),
    (12, 0, -2, 0), (18, 0, -1, 0), (19, 0, 0, 1), (8, 1, 1, -1), (21, 0, 0, -1), (26, 0, -1, 0), (13, 0, 1, 0),
    (14, 0, 0, -1), (27, 0, 0, -1), (18, -1, 0, 0), (28, 0, 0, -1), (17, 0, 0, 1), (23, 0, 1, 0), (19, 1, 0, 0),
    (21, -1, 0, 0), (22, -1, 0, 0), (23, 1, 0, 0), (27, 0, 0, 1), (27, -1, 0, 0), (27, 0, -1, 0), (30, 0, 0, 1),
    (29, 0, 1, 0), (24, 1, 1, 0), (28, -1, 0, 0), (28, 0, -1, 0), (32, 0, 0, 1), (32, 1, 0, 0), (35, 0, 0, -1),
    (24, 0, 2, 0), (33, 1, 0, 0), (34, 0, 1, 0), (32, 0, -1, 0), (41, -1, 0, 0), (39, 0, 0, 1), (36, 1, 0, 0),
    (39, 0, 1, 0), (44, 0, 0, -1), (35, 0, -1, 0), (38, 1, 0, 0), (46, 0, 1, 0), (35, -1, 0, 1), (30, 0, -1, 1),
    (36, 0, -1, 0), (46, -1, 0, 0), (40, 0, 0, 1), (52, 1, 0, 0), (52, 0, 0, -1), (52, 0, 1, 0), (37, 0, -1, 0),
    (54, -1, 0, 0), (48, 0, 0, 1), (53, 0, 0, -1), (54, 0, 1, 0), (56, 1, 0, 0), (45, 0, -1, 0), (58, -1, 0, 0),
    (52, 0, 0, 1), (55, 0, 0, -1), (55, 0, 1, 0), (57, 1, 0, 0), (49, 0, -1, 0), (61, -1, 0, 0), (57, 0, 0, 1),
    (60, 0, 0, -1), (57, 0, 1, 0), (65, 1, 0, 0), (62, 0, -1, 0), (59, 0, 0, 1), (65, 0, 0, -1), (60, 0, 1, 0),
    (67, 1, 0, 0),
)
SENDS = (
    4, 6, 1, 8, 2, 5, 3, 7, 12, 9, 10, 19, 11, 20, 14, 13, 25, 28, 15, 16, 24, 31, 17, 27, 43, 18, 32, 42, 21, 47,
    35, 23, 41, 26, 50, 22, 60, 29, 51, 34, 36, 30, 33, 37, 38, 40, 39, 52, 57, 63, 64, 54, 46, 48, 49, 44, 45, 53,
    68, 66, 58, 55, 59, 56, 70, 61, 71, 72, 69, 73, 79, 85, 62, 65, 75, 74, 76, 67, 81, 80, 78, 98, 77, 82, 88, 83,
    86, 87, 94, 97, 84, 91, 99, 105, 95, 90, 92, 101, 89, 93, 111, 100, 96, 107, 117, 113, 102, 103, 104, 108, 106,
    109, 114, 115, 110, 119, 116, 121, 112, 124, 126, 120, 118, 123, 122, 125, 127,
)


def total_steps():
    ways = [(0, 0, 0)]
    for source, *jump in STEPS:
        ways.append(tuple(a + b for a, b in zip(ways[source], jump)))
    after = [[] for way in ways]
    for number in SENDS:
        source, *jump = STEPS[number - 1]
        after[source].append((number, tuple(jump)))
    return ways, after


def pair_tables():
    k = np.arange(STRETCH, dtype=np.float64)[:, None]
    n = np.arange(STRETCH, dtype=np.float64)[None, :]
    scale = np.where(k == 0, math.sqrt(1.0 / STRETCH), math.sqrt(2.0 / STRETCH))
    cosine = np.kron(np.eye(2), scale * np.cos(math.pi * (2.0 * n + 1.0) * k / (2.0 * STRETCH)))

    return np.stack([cosine.T, cosine]).astype(np.float32)


def iota(shape, dim):
    return lax.broadcasted_iota(jnp.int32, shape, dim)


def lane_gather(values, lanes):
    return jnp.take_along_axis(values, lanes, axis=1, mode="promise_in_bounds")


def split(values):
    high = values.astype(jnp.bfloat16)
    low = (values - high.astype(jnp.float32)).astype(jnp.bfloat16)
    return jnp.concatenate([high, low], axis=1)


def table_dot(rows, table):
    both = jnp.dot(
        split(rows),
        jnp.concatenate([table, table], axis=0),
        preferred_element_type=jnp.float32,
    )
    return both[:, :128] + both[:, 128:]


def sync_kernel(momentum_in, gradients_in, weight_in, indices_in, tables_in, moment_out, whole,
                momentum, gradients, weight, indices, tables, kept_columns, message, inbox, loaded,
                list_sent, list_here, passed_on, here, twin_sent, twin_here):
    dp = lax.axis_index("dp")
    fsdp = lax.axis_index("fsdp")
    z, x = lax.div(dp, NX), lax.rem(dp, NX)
    y, core = lax.div(fsdp, 2), lax.rem(fsdp, 2)
    colour = lax.rem(2 * x + y + 3 * z, COLOURS)
    odd = lax.rem(x, 2)
    parities = [odd, 1 - odd]
    xs = [lax.rem(x + d, NX) for d in range(NX)]
    ys = [lax.rem(y + d, NY) for d in range(NY)]
    zs = [lax.rem(z + d, NZ) for d in range(NZ)]
    tints = [lax.rem(colour + d, COLOURS) for d in range(COLOURS)]

    def chip(dx, dy, dz):
        return (zs[dz % NZ] * NX + xs[dx % NX], ys[dy % NY] * 2 + core)

    twin = (dp, y * 2 + 1 - core)

    own_rows = pl.ds(pl.multiple_of(colour * ROWS + odd * HALF, HALF), HALF)
    first, second = pl.ds(0, COLOURS // 2 * ROWS), pl.ds(COLOURS // 2 * ROWS, COLOURS // 2 * ROWS)
    loads = [
        pltpu.make_async_copy(source, target, loaded.at[number])
        for number, (source, target) in enumerate((
            (indices_in, indices), (tables_in, tables),
            (momentum_in.at[first], momentum.at[first]), (gradients_in.at[first], gradients.at[first]),
            (momentum_in.at[second], momentum.at[second]), (gradients_in.at[second], gradients.at[second]),
            (weight_in.at[own_rows], weight),
        ))
    ]
    for load in loads:
        load.start()

    plane = [(dx, dz) for dz in (0, 1, 7, 2, 6, 3, 5, 4) for dx in (0, 1, 3, 2) if (dx, dz) != (0, 0)]
    barrier = pltpu.get_barrier_semaphore()
    ways, after = total_steps()
    others = sorted({(dx % NX, dy % NY, dz % NZ) for source, dx, dy, dz in STEPS if dy != 0})
    senders = [(-dx, -dy, -dz) for dx, dy, dz in others] + [(dx, 0, dz) for dx, dz in plane]
    senders.sort(key=lambda step: -sum(min(d % n, -d % n) for d, n in zip(step, (NX, NY, NZ))))
    for step in senders:
        pl.semaphore_signal(barrier, 1, device_id=chip(*step))
    pl.semaphore_signal(barrier, 1, device_id=twin)

    lane = iota((8, 128), 1)
    even = iota((TOPK, 128), 1) % 2 == 0
    component = iota((STRETCH, 128), 0)
    front = iota((TOPK, 128), 1) < HALF

    for load in loads[:4]:
        load.wait()

    forward, backward = split(tables[0]), split(tables[1])

    def driven_rows(rows):
        return decay_rate * momentum[rows, :] + gradients[rows, :].astype(jnp.float32)

    def transform(share, carry):
        rows = pl.ds(pl.multiple_of(share * ROWS, ROWS), ROWS)
        columns = table_dot(driven_rows(rows), forward).T
        listed = jnp.concatenate([indices[0, :, rows], indices[1, :, rows]], axis=0)
        below = lane_gather(listed, (lane + 127) % 128)
        above = lane_gather(listed, (lane + 1) % 128)
        places = (
            jnp.where(even, listed[:TOPK], below[TOPK:]),
            jnp.where(even, above[:TOPK], listed[TOPK:]),
        )
        picked = []
        for half in range(2):
            part = columns[STRETCH * half : STRETCH * (half + 1)]
            kept = jnp.zeros((STRETCH, 128), jnp.float32)
            for slot in range(TOPK):
                match = component == places[half][slot : slot + 1]
                picked.append(jnp.sum(jnp.where(match, part, 0.0), axis=0, keepdims=True))
                kept = jnp.where(match, part, kept)
            kept_columns[share, pl.ds(STRETCH * half, STRETCH), :] = kept
        for number, rows_of in enumerate((jnp.concatenate(picked, axis=0), jnp.concatenate(places, axis=0))):
            turned = lane_gather(rows_of, (lane + HALF) % 128)
            tiles = (
                jnp.where(front, rows_of[:TOPK], turned[TOPK:]),
                jnp.where(front, turned[:TOPK], rows_of[TOPK:]),
            )
            for half in range(2):
                tile = tiles[half]
                if number == 0:
                    message[2 * share + half, 0] = tile[:2]
                    message[2 * share + half, 1] = tile[2:]
                else:
                    message[2 * share + half, 2] = (tile[:2] + 65536 * tile[2:]).astype(jnp.float32)
        return carry

    lax.fori_loop(0, COLOURS // 2, transform, 0, unroll=4)
    for load in loads[4:6]:
        load.wait()
    lax.fori_loop(COLOURS // 2, COLOURS, transform, 0, unroll=4)

    pl.semaphore_wait(barrier, len(plane) + len(others) + 1)

    for number, (dx, dz) in reversed(list(enumerate(plane))):
        pltpu.make_async_remote_copy(
            src_ref=message.at[2 * tints[(2 * dx + 3 * dz) % COLOURS] + parities[dx % 2]], dst_ref=inbox.at[number], send_sem=list_sent,
            recv_sem=list_here.at[number], device_id=chip(dx, 0, dz),
        ).start()

    def keep_rest(share, carry):
        rows = pl.ds(pl.multiple_of(share * ROWS, ROWS), ROWS)
        moment_out[rows, :] = driven_rows(rows) - table_dot(kept_columns[share].T, backward)
        return carry

    lax.fori_loop(0, COLOURS, keep_rest, 0)

    def list_sum(tile):
        coded = tile[2].astype(jnp.int32)
        places = (coded % 65536, coded // 65536)
        term = jnp.zeros((STRETCH, 128), jnp.float32)
        for slot in range(TOPK):
            match = component == places[slot // 2][slot % 2 : slot % 2 + 1]
            term = jnp.where(match, tile[slot // 2, pl.ds(slot % 2, 1), :], term)
        return term

    def add_list(number, summed):
        pltpu.make_async_copy(inbox.at[number], inbox.at[number], list_here.at[number]).wait()
        return summed + list_sum(inbox.at[number])

    summed = lax.fori_loop(0, len(plane), add_list, list_sum(message.at[2 * colour + odd]))
    turned = lane_gather(summed, (iota((STRETCH, 128), 1) + HALF) % 128)
    restored = table_dot(jnp.concatenate([summed, turned], axis=0).T[:HALF], backward)
    loads[6].wait()
    whole[y, core, colour, odd] = (weight[...].astype(jnp.float32) - rate_step * restored).astype(jnp.bfloat16)

    def block(plane, tint, half):
        return whole.at[plane, core, tint, half]

    def send(what, sent, here, where):
        pltpu.make_async_remote_copy(
            src_ref=what, dst_ref=what, send_sem=sent, recv_sem=here, device_id=where
        ).start()

    def have(number):
        dx, dy, dz = ways[number]
        what = block(ys[-dy % NY], tints[-(2 * dx + dy + 3 * dz) % COLOURS], parities[dx % 2])
        if number > 0:
            pltpu.make_async_copy(what, what, here.at[number]).wait()
        for follower, step in after[number]:
            send(what, passed_on.at[(sent[0] >= 112) + (sent[0] >= 126)], here.at[follower], chip(*step))
            sent[0] += 1
        send(what, twin_sent, twin_here, twin)

    sent = [0]
    for number in range(len(ways)):
        have(number)

    def await_bytes(ref, semaphore):
        pltpu.make_async_copy(ref, ref, semaphore).wait()

    await_bytes(inbox, list_sent)
    await_bytes(whole.at[pl.ds(0, 7), core], passed_on.at[0])
    await_bytes(whole.at[0, core, pl.ds(0, 7)], passed_on.at[1])
    await_bytes(whole.at[0, core, 7, 0], passed_on.at[2])
    await_bytes(whole.at[:, core], twin_sent)
    await_bytes(whole.at[:, 1 - core], twin_here)


def settle_kernel(moment_rows, whole, moment_out, weight_out, written):
    copies = [pltpu.make_async_copy(moment_rows, moment_out, written.at[NY])]
    for plane in range(NY):
        copies.append(pltpu.make_async_copy(whole.at[plane], weight_out.at[plane], written.at[plane]))
    for copy in copies:
        copy.start()
    for copy in copies:
        copy.wait()


def as_rows(array):
    layers, entries = array.shape
    return array.reshape(layers, entries // 128, 128).transpose(1, 0, 2).reshape(layers * entries // 128, 128)


def from_rows(array, layers):
    pieces = array.shape[0] // layers
    return array.reshape(pieces, layers, 128).transpose(1, 0, 2).reshape(layers, pieces * 128)


def shards(momentum, gradients, weight, indices):
    layers, entries = weight.shape
    rows = layers * entries // 128
    in_hbm = pl.BlockSpec(memory_space=pltpu.HBM)
    in_vmem = pl.BlockSpec(memory_space=pltpu.VMEM)
    dma = pltpu.SemaphoreType.DMA
    peers = NX * NZ - 1
    operands = (
        as_rows(momentum[0]), as_rows(gradients[0]), as_rows(weight), indices[0], jnp.asarray(pair_tables())
    )
    moment_rows, whole = pl.pallas_call(
        sync_kernel,
        out_shape=(
            jax.ShapeDtypeStruct((rows, 128), jnp.float32),
            jax.ShapeDtypeStruct((NY, 2, COLOURS, 2, HALF, 128), jnp.bfloat16),
        ),
        in_specs=[in_hbm] * 5,
        out_specs=(in_vmem, in_vmem),
        scratch_shapes=[
            pltpu.VMEM((rows, 128), jnp.float32),
            pltpu.VMEM((rows, 128), jnp.bfloat16),
            pltpu.VMEM((HALF, 128), jnp.bfloat16),
            pltpu.VMEM(indices.shape[1:], jnp.int32),
            pltpu.VMEM((2, 128, 128), jnp.float32),
            pltpu.VMEM((COLOURS, 128, ROWS), jnp.float32),
            pltpu.VMEM((2 * COLOURS, 3, 2, 128), jnp.float32),
            pltpu.VMEM((peers, 3, 2, 128), jnp.float32),
            dma((7,)), dma, dma((peers,)), dma((3,)), dma((len(STEPS) + 1,)), dma, dma,
        ],
        compiler_params=pltpu.CompilerParams(
            collective_id=0, has_side_effects=True, vmem_limit_bytes=24 * 2**20
        ),
    )(*(pltpu.with_memory_space_constraint(operand, pltpu.HBM) for operand in operands))
    moment_rows, whole = pl.pallas_call(
        settle_kernel,
        out_shape=(
            jax.ShapeDtypeStruct(moment_rows.shape, jnp.float32),
            jax.ShapeDtypeStruct(whole.shape, jnp.bfloat16),
        ),
        in_specs=[in_vmem] * 2,
        out_specs=(in_hbm, in_hbm),
        scratch_shapes=[dma((NY + 1,))],
        compiler_params=pltpu.CompilerParams(vmem_limit_bytes=8 * 2**20),
    )(moment_rows, whole)
    weight_out = from_rows(whole.reshape(-1, 128), layers)
    return (from_rows(moment_rows, layers)[None], weight_out)


def solution(mesh):
    return jax.shard_map(
        shards,
        mesh=mesh,
        in_specs=(
            P("dp", None, "fsdp"),
            P("dp", None, "fsdp"),
            P(None, "fsdp"),
            P("dp", None, None, "fsdp"),
        ),
        out_specs=(P("dp", None, "fsdp"), P()),
        check_vma=False,
    )
```
